32 devices in a mesh: parts: 2 (over y), nest: 4 (over z), tx: 4 (over x, core).
Axes of the slice: x: 2, y: 2, z: 4, core: 2. Of those that a mesh axis runs over, the one named last changes fastest.
Arguments:
- model_state: float32 [96, 256, 512], P('parts', 'nest', 'tx'), parts along dimension 0, may hold values from -6 to 6
- diffusivity: float32 [512, 512], P(('parts', 'nest'), 'tx'), parts along dimension 0, may hold values from 0.05 to 0.24
- rim_index: int32 [16, 512], P('nest', 'tx'), may hold values from 0 to 4095
- rim_weight: float32 [16, 512], P('nest', 'tx'), may hold values from 0.05 to 0.5
- side_index: int32 [16, 128], P('nest'), may hold values from 0 to 4095
- side_weight: float32 [16, 128], P('nest'), may hold values from 0.05 to 0.5
- rim_tile: int32 [4, 4], P('nest', 'tx'), may hold values from 0 to 1
- nest_offset: int32 [2], replicated, may hold values from 0 to 4095
Outputs:
- new_state: float32 [96, 256, 512], P('parts', 'nest', 'tx'), parts along dimension 0
The draws below stay inside these ranges and needn't reach their ends.
There are 2 independent parts, one for each index of `parts`. The reference program is written for one: setup_inputs(seed, part) draws one part's arguments, and reference() takes and returns one part's arrays. A program takes and returns all parts, laid end to end along the dimension named above; an argument that names none is the same for every part. Nothing has to cross between parts.
Inputs may be any that keep to these rules, and one draw needn't show every extreme that they name: Sources are counted from their grid's offset: rim_index plus nest_offset of its grid stays below 8192. Sources are counted from their grid's offset: side_index plus nest_offset of its grid stays below 8192. `nest_offset`: the parent's entry is not read.
All inputs are finite; a program needn't handle non-finite values.
Results may differ from the reference program's by a relative error of at most 0.0001.
Values sent between devices are 32-bit elements; how exact they have to be, the bound alone decides.
A program may use at most 128 MiB of HBM per device.

```python
import jax
import jax.numpy as jnp
from jax import lax

VARS = 48
RD = 64
CD = 128
STEPS = 2
GROUPS = 2
ROWS = 256
COLS = 512
N_NEST = 4
N_TX = 4


def set_ends(result, stream_key, smallest, high):
    dims = result.shape
    spot = [jax.random.randint(jax.random.fold_in(stream_key, axis), (), 0, dims[axis]) for axis in range(len(dims))]
    result = result.at[tuple(spot)].set(smallest)
    longest = dims.index(max(dims))
    spot[longest] = (spot[longest] + 1) % dims[longest]
    return result.at[tuple(spot)].set(high)


def level_of(stream_key, extent, split, smallest, largest):
    def one(axis_at, blocks):
        steps = jax.random.uniform(jax.random.fold_in(jax.random.fold_in(stream_key, 6), axis_at), (blocks,), jnp.float32, smallest / len(split), largest / len(split))
        return jnp.repeat(jnp.exp(steps), extent[axis_at] // blocks).reshape((-1,) + (1,) * (len(extent) - axis_at - 1))

    level = one(*split[0])
    for cut in split[1:]:
        level = level * one(*cut)
    return level


def scatter_about(own_key, extent, spread, reach, pieces=(), dtype=jnp.bfloat16):
    loudness = level_of(own_key, extent, pieces, -0.22, 0.18) if pieces else 1.0
    entries = jax.random.normal(own_key, extent, jnp.float32) * spread * loudness
    return jnp.minimum(jnp.maximum(entries, -reach), reach).astype(dtype)


def setup_inputs(seed: int = 0, part: int = 0) -> dict:
    keys = jax.random.split(jax.random.key(seed), 9)
    part_splits = jax.random.split(jax.random.fold_in(keys[8], part), 9)
    return {
        "model_state": scatter_about(part_splits[0], (VARS, ROWS, COLS), 1.0, 6.0, ((1, 4), (2, 4)), jnp.float32),
        "diffusivity": jnp.clip(0.05 + 0.19 * jax.random.uniform(part_splits[1], (ROWS, COLS), jnp.float32) ** level_of(part_splits[1], (ROWS, COLS), ((0, 4), (1, 4)), -0.2, 0.2), 0.05, 0.24),
        "rim_index": set_ends(jax.random.randint(keys[2], (N_NEST * 4, COLS), 0, RD * CD // 2), jax.random.fold_in(keys[2], 1), 0, (RD * CD // 2) - 1).astype(jnp.int32),
        "rim_weight": jnp.clip(0.05 + 0.45 * jax.random.uniform(keys[3], (N_NEST * 4, COLS), jnp.float32) ** level_of(keys[3], (N_NEST * 4, COLS), ((0, 4), (1, 4)), -0.2, 0.2), 0.05, 0.5),
        "side_index": set_ends(jax.random.randint(keys[4], (N_NEST * 4, 2 * RD), 0, RD * CD // 2), jax.random.fold_in(keys[4], 1), 0, (RD * CD // 2) - 1).astype(jnp.int32),
        "side_weight": jnp.clip(0.05 + 0.45 * jax.random.uniform(keys[5], (N_NEST * 4, 2 * RD), jnp.float32) ** level_of(keys[5], (N_NEST * 4, 2 * RD), ((0, 4),), -0.2, 0.2), 0.05, 0.5),
        "rim_tile": set_ends(jax.random.randint(keys[6], (N_NEST, N_TX), 0, 2), jax.random.fold_in(keys[6], 1), 0, 1).astype(jnp.int32),
        "nest_offset": jax.random.randint(keys[7], (GROUPS,), 0, RD * CD // 2).astype(jnp.int32),
    }


def interpolate(flat_tile, flat_index, weights):
    picked = jnp.take(flat_tile, flat_index.reshape(-1), axis=1)
    picked = picked.reshape((flat_tile.shape[0],) + flat_index.shape)
    return jnp.sum(picked * weights[None], axis=-2)


def reference(model_state, diffusivity, rim_index, rim_weight, side_index, side_weight, rim_tile, nest_offset):
    fields = model_state
    device_ids = jnp.arange(N_NEST)
    offsets = nest_offset[device_ids // 2]
    index_blocks = rim_index.reshape(N_NEST, 4, N_TX, CD).transpose(0, 2, 1, 3)
    weight_blocks = rim_weight.reshape(N_NEST, 4, N_TX, CD).transpose(0, 2, 1, 3)
    side_blocks = side_index.reshape(N_NEST, 4, 2 * RD)
    side_wblocks = side_weight.reshape(N_NEST, 4, 2 * RD)
    column_ids = jnp.arange(N_TX)
    even = (device_ids % 2 == 0)[None, :, None]
    parent = (device_ids < 2)[None, :, None]
    row_parent = (jnp.arange(ROWS) < 2 * RD)[None]
    for step_index in range(STEPS):
        parent_tiles = fields[:, :2 * RD].reshape(VARS, 2, RD, N_TX, CD).transpose(1, 3, 0, 2, 4).reshape(2, N_TX, VARS, RD * CD)

        def device_rims(inputs):
            tile_row, index_row, weight_row, offset = inputs
            sources = parent_tiles[tile_row, column_ids]
            return jax.vmap(interpolate)(sources, index_row + offset, weight_row)

        def device_sides(inputs):
            tile_row, index_row, weight_row, offset = inputs
            left_vals = interpolate(parent_tiles[tile_row[0], 0], index_row[:, :RD] + offset, weight_row[:, :RD])
            right_vals = interpolate(parent_tiles[tile_row[N_TX - 1], N_TX - 1], index_row[:, RD:] + offset, weight_row[:, RD:])
            return left_vals, right_vals

        rims = lax.map(device_rims, (rim_tile, index_blocks, weight_blocks, offsets))
        lefts, rights = lax.map(device_sides, (rim_tile, side_blocks, side_wblocks, offsets))
        left_cols = lefts.transpose(1, 0, 2).reshape(VARS, ROWS)
        right_cols = rights.transpose(1, 0, 2).reshape(VARS, ROWS)
        rim_rows = rims.transpose(2, 0, 1, 3).reshape(VARS, N_NEST, N_TX * CD)
        blocks = fields.reshape(VARS, N_NEST, RD, N_TX * CD)
        first_rows = blocks[:, :, 0]
        last_rows = blocks[:, :, -1]
        top_ghost = jnp.where(even, jnp.where(parent, first_rows, rim_rows), jnp.roll(last_rows, 1, axis=1))
        bottom_ghost = jnp.where(even, jnp.roll(first_rows, -1, axis=1), jnp.where(parent, last_rows, rim_rows))
        above = jnp.concatenate([top_ghost[:, :, None], blocks[:, :, :-1]], axis=2).reshape(fields.shape)
        below_rows = jnp.concatenate([blocks[:, :, 1:], bottom_ghost[:, :, None]], axis=2).reshape(fields.shape)
        left_side = jnp.roll(fields, 1, axis=2)
        left_side = left_side.at[:, :, 0].set(jnp.where(row_parent, left_side[:, :, 0], left_cols))
        right_side = jnp.roll(fields, -1, axis=2)
        right_side = right_side.at[:, :, -1].set(jnp.where(row_parent, right_side[:, :, -1], right_cols))
        laplace = above + below_rows + left_side + right_side - 4.0 * fields
        fields = fields + diffusivity[None] * laplace
    return fields
```

```python
import functools

import jax
import jax.numpy as jnp
from jax import lax
from jax.experimental import pallas as pl
from jax.experimental.pallas import tpu as pltpu
from jax.sharding import PartitionSpec as P

STEPS = 2
MESH = pl.DeviceIdType.MESH


def kernel(
    blocks,
    columns,
    state_hbm,
    diff_ref,
    rim_index_ref,
    rim_weight_ref,
    side_index_ref,
    side_weight_ref,
    tile_ref,
    offset_ref,
    out_hbm,
    u0,
    u1,
    u2,
    idx_send,
    w_send,
    idx_recv,
    w_recv,
    row_weights,
    col_send,
    col_recv,
    halo,
    row_send,
    row_recv,
    outer,
    rim_out,
    rim_recv,
    side_rows,
    side_out,
    side_recv,
    load_sem,
    store_sem,
    param_send_sem,
    param_recv_sem,
    col_send_sem,
    col_recv_sem,
    row_send_sem,
    row_recv_sem,
    rim_send_sem,
    rim_recv_sem,
    side_send_sem,
    side_recv_sem,
):
    var_count, tile_rows, tile_cols = u0.shape
    groups = tile_rows // 8
    nests = blocks - 2
    me = lax.axis_index("nest")
    t = lax.axis_index("tx")
    right, left = lax.rem(t + 1, columns), lax.rem(t + columns - 1, columns)
    parity = lax.rem(me, 2)
    mate = me + 1 - 2 * parity
    is_parent = me < 2
    is_nest = me >= 2
    at_edge = jnp.logical_or(t == 0, t == columns - 1)

    load = pltpu.make_async_copy(state_hbm, u0, load_sem)
    load.start()

    barrier = pltpu.get_barrier_semaphore()
    pl.semaphore_signal(barrier, inc=1, device_id={"tx": left}, device_id_type=MESH)
    pl.semaphore_signal(barrier, inc=1, device_id={"tx": right}, device_id_type=MESH)
    pl.semaphore_signal(barrier, inc=1, device_id={"nest": mate}, device_id_type=MESH)

    @pl.when(is_nest)
    def _():
        for p in range(2):
            pl.semaphore_signal(barrier, inc=1, device_id={"nest": p}, device_id_type=MESH)
        pl.semaphore_wait(barrier, 5)

    @pl.when(is_parent)
    def _():
        for b in range(nests):
            pl.semaphore_signal(barrier, inc=1, device_id={"nest": 2 + b}, device_id_type=MESH)
        pl.semaphore_wait(barrier, 3 + nests)

    row_id = lax.broadcasted_iota(jnp.int32, (tile_rows, tile_cols), 0)
    lane = lax.broadcasted_iota(jnp.int32, (tile_rows, tile_cols), 1)
    lane8 = lax.broadcasted_iota(jnp.int32, (8, tile_cols), 1)
    half = tile_rows

    def param_copies(p, slot):
        return (
            pltpu.make_async_remote_copy(
                src_ref=idx_send,
                dst_ref=idx_recv.at[slot],
                send_sem=param_send_sem.at[0, p],
                recv_sem=param_recv_sem.at[0, slot],
                device_id={"nest": p},
                device_id_type=MESH,
            ),
            pltpu.make_async_remote_copy(
                src_ref=w_send.at[p],
                dst_ref=w_recv.at[slot],
                send_sem=param_send_sem.at[1, p],
                recv_sem=param_recv_sem.at[1, slot],
                device_id={"nest": p},
                device_id_type=MESH,
            ),
        )

    @pl.when(is_nest)
    def _():
        offset = offset_ref[me // 2]
        tile = tile_ref[0, 0]
        stay = (t == 0) == (parity == 0)
        index = side_index_ref[...]
        weight = side_weight_ref[...]
        turned_index = jnp.concatenate([index[:, half:], index[:, :half]], axis=1)
        turned_weight = jnp.concatenate([weight[:, half:], weight[:, :half]], axis=1)
        idx_send[0:4] = rim_index_ref[...] + offset
        idx_send[4:8] = jnp.where(stay, index, turned_index) + offset
        for p in range(2):
            keep = jnp.where(tile == p, 1.0, 0.0)
            w_send[p, 0:4] = rim_weight_ref[...] * keep
            w_send[p, 4:8] = jnp.where(stay, weight, turned_weight) * keep
        for p in range(2):
            for copy in param_copies(p, me - 2):
                copy.start()

    load.wait()

    def col_copies(step):
        return (
            pltpu.make_async_remote_copy(
                src_ref=col_send.at[step],
                dst_ref=col_recv.at[step, 0],
                send_sem=col_send_sem.at[step, 0],
                recv_sem=col_recv_sem.at[step, 0],
                device_id={"tx": right},
                device_id_type=MESH,
            ),
            pltpu.make_async_remote_copy(
                src_ref=col_send.at[step],
                dst_ref=col_recv.at[step, 1],
                send_sem=col_send_sem.at[step, 1],
                recv_sem=col_recv_sem.at[step, 1],
                device_id={"tx": left},
                device_id_type=MESH,
            ),
            pltpu.make_async_remote_copy(
                src_ref=row_send.at[step],
                dst_ref=row_recv.at[step],
                send_sem=row_send_sem.at[step],
                recv_sem=row_recv_sem.at[step],
                device_id={"nest": mate},
                device_id_type=MESH,
            ),
        )

    def take_edges(step, v, tile, packed):
        last, first = tile[tile_rows - 1 :], tile[:1]
        row_send[step, pl.ds(v, 1), :] = jnp.where(parity == 0, last, first)

        @pl.when(is_parent)
        def _():
            outer[pl.ds(v, 1), :] = jnp.where(parity == 0, first, last)

        return jnp.where(lane // 2 == v, pltpu.roll(tile, 2 * v + 1, 1), packed)

    zeros = jnp.zeros((tile_rows, tile_cols), jnp.float32)
    col_send[0] = lax.fori_loop(0, var_count, lambda v, packed: take_edges(0, v, u0[v], packed), zeros)
    for copy in col_copies(0):
        copy.start()

    def rim_copies(step, slot, p):
        return pltpu.make_async_remote_copy(
            src_ref=rim_out.at[step, slot],
            dst_ref=rim_recv.at[step, p],
            send_sem=rim_send_sem.at[step, slot],
            recv_sem=rim_recv_sem.at[step, p],
            device_id={"nest": 2 + slot},
            device_id_type=MESH,
        )

    def side_copies(step, slot, p):
        return pltpu.make_async_remote_copy(
            src_ref=side_out.at[step, slot],
            dst_ref=side_recv.at[step, p],
            send_sem=side_send_sem.at[step, slot],
            recv_sem=side_recv_sem.at[step, p],
            device_id={"nest": 2 + slot},
            device_id_type=MESH,
        )

    def gather(vector, index):
        return jnp.take_along_axis(vector, index, axis=1, mode="promise_in_bounds")

    def column_of(row):
        return jnp.broadcast_to(lax.rem(row, tile_cols), (8, tile_cols))

    def weights_of(index, weight):
        return jnp.where(row_id == index // tile_cols, weight, 0.0)

    def side_rows_of(pair):
        low = lane8[:4] < half
        index = jnp.where(low, idx_recv[2 * pair, 4:8], idx_recv[2 * pair + 1, 4:8])
        weight = jnp.where(low, w_recv[2 * pair, 4:8], w_recv[2 * pair + 1, 4:8])
        return index, weight

    def sets_of(pair, what):
        if what == 2:
            return side_rows_of(pair)
        return idx_recv[2 * pair + what, 0:4], w_recv[2 * pair + what, 0:4]

    def prepare():
        for slot in range(nests):
            for p in range(2):
                @pl.when(me == p)
                def _():
                    for copy in param_copies(p, slot):
                        copy.wait_recv()
        for pair in range(nests // 2):
            for what in range(3):
                index, weight = sets_of(pair, what)
                for k in range(4):
                    row_weights[pair, what, k] = weights_of(index[k : k + 1], weight[k : k + 1])

    def interpolate(step, source):
        for pair in range(nests // 2):

            def run(whats):
                columns_of = {
                    (what, k): column_of(sets_of(pair, what)[0][k : k + 1]) for what in whats for k in range(4)
                }

                def one(v, carry):
                    totals = {what: jnp.zeros((8, tile_cols), jnp.float32) for what in whats}
                    for g in range(groups):
                        cells = source[v, 8 * g : 8 * g + 8, :]
                        for what in whats:
                            for k in range(4):
                                totals[what] += (
                                    gather(cells, columns_of[what, k]) * row_weights[pair, what, k, 8 * g : 8 * g + 8]
                                )
                    for what in whats:
                        value = jnp.sum(totals[what], axis=0, keepdims=True)
                        if what == 2:
                            side_rows[pl.ds(2 * v, 1), :] = value
                            side_rows[pl.ds(2 * v + 1, 1), :] = value
                        else:
                            rim_out[step, 2 * pair + what, pl.ds(v, 1), :] = value
                    return carry

                lax.fori_loop(0, var_count, one, 0)

            @pl.when(at_edge)
            def _():
                run((0, 1, 2))
                turned = side_rows[...].T
                for what in range(2):
                    side_out[step, 2 * pair + what] = turned[what * half : (what + 1) * half]
                for what in range(2):
                    for p in range(2):
                        @pl.when(me == p)
                        def _():
                            side_copies(step, 2 * pair + what, p).start()

            @pl.when(jnp.logical_not(at_edge))
            def _():
                run((0, 1))

            for what in range(2):
                for p in range(2):
                    @pl.when(me == p)
                    def _():
                        rim_copies(step, 2 * pair + what, p).start()

    @pl.when(is_parent)
    def _():
        side_rows[...] = jnp.zeros_like(side_rows)
        prepare()
        interpolate(0, u0)

    diffusivity = diff_ref

    for step in range(STEPS):
        source, target = ((u0, u1), (u1, u2))[step]
        to_right, to_left, to_mate = col_copies(step)
        to_right.wait_recv()
        to_left.wait_recv()
        to_mate.wait_recv()
        halo[...] = jnp.where(lane % 2 == 0, col_recv[step, 0], col_recv[step, 1])

        @pl.when(is_nest)
        def _():
            for p in range(2):
                rim_copies(step, 0, p).wait_recv()
            outer[...] = rim_recv[step, 0] + rim_recv[step, 1]

            @pl.when(at_edge)
            def _():
                for p in range(2):
                    side_copies(step, 0, p).wait_recv()
                own = lane % 2 == jnp.where(t == 0, 0, 1)
                halo[...] = jnp.where(own, side_recv[step, 0] + side_recv[step, 1], halo[...])

        def one(v, packed):
            u = source[v]
            mate_row = row_recv[step, pl.ds(v, 1), :]
            outer_row = outer[pl.ds(v, 1), :]
            top = jnp.where(parity == 0, outer_row, mate_row)
            bottom = jnp.where(parity == 0, mate_row, outer_row)
            ghost = pltpu.roll(halo[...], tile_cols - 1 - 2 * v, 1)
            left_side = pltpu.roll(jnp.where(lane == tile_cols - 1, ghost, u), 1, 1)
            right_side = pltpu.roll(jnp.where(lane == 0, ghost, u), tile_cols - 1, 1)
            above = jnp.where(row_id == 0, top, pltpu.roll(u, 1, 0))
            below = jnp.where(row_id == tile_rows - 1, bottom, pltpu.roll(u, tile_rows - 1, 0))
            laplace = above + below + left_side + right_side - 4.0 * u
            new = u + diff_ref[...] * laplace
            target[v] = new
            if step + 1 < STEPS:
                return take_edges(step + 1, v, new, packed)
            return packed

        packed = lax.fori_loop(0, var_count, one, zeros)
        if step + 1 < STEPS:
            col_send[step + 1] = packed
            for copy in col_copies(step + 1):
                copy.start()

            @pl.when(is_parent)
            def _():
                interpolate(step + 1, target)

    store = pltpu.make_async_copy(u2, out_hbm, store_sem)
    store.start()

    for step in range(STEPS):
        for copy in col_copies(step):
            copy.wait_send()

    @pl.when(is_nest)
    def _():
        for p in range(2):
            for copy in param_copies(p, 0):
                copy.wait_send()

    @pl.when(is_parent)
    def _():
        for step in range(STEPS):
            for slot in range(nests):
                rim_copies(step, slot, 0).wait_send()

                @pl.when(at_edge)
                def _():
                    side_copies(step, slot, 0).wait_send()

    store.wait()


def per_device(mesh_shape, *arrays):
    model_state = arrays[0]
    var_count, tile_rows, tile_cols = model_state.shape
    blocks, columns = mesh_shape["nest"], mesh_shape["tx"]
    nests = blocks - 2
    f32 = jnp.float32
    tile = (tile_rows, tile_cols)
    rows = (var_count, tile_cols)
    vmem = pl.BlockSpec(memory_space=pltpu.VMEM)
    smem = pl.BlockSpec(memory_space=pltpu.SMEM)
    hbm = pl.BlockSpec(memory_space=pl.ANY)
    dma = pltpu.SemaphoreType.DMA
    return pl.pallas_call(
        functools.partial(kernel, blocks, columns),
        out_shape=jax.ShapeDtypeStruct(model_state.shape, f32),
        in_specs=[hbm, vmem, vmem, vmem, vmem, vmem, smem, smem],
        out_specs=hbm,
        scratch_shapes=[
            pltpu.VMEM(model_state.shape, f32),
            pltpu.VMEM(model_state.shape, f32),
            pltpu.VMEM(model_state.shape, f32),
            pltpu.VMEM((8, tile_cols), jnp.int32),
            pltpu.VMEM((2, 8, tile_cols), f32),
            pltpu.VMEM((nests, 8, tile_cols), jnp.int32),
            pltpu.VMEM((nests, 8, tile_cols), f32),
            pltpu.VMEM((nests // 2, 3, 4) + tile, f32),
            pltpu.VMEM((STEPS,) + tile, f32),
            pltpu.VMEM((STEPS, 2) + tile, f32),
            pltpu.VMEM(tile, f32),
            pltpu.VMEM((STEPS,) + rows, f32),
            pltpu.VMEM((STEPS,) + rows, f32),
            pltpu.VMEM(rows, f32),
            pltpu.VMEM((STEPS, nests) + rows, f32),
            pltpu.VMEM((STEPS, 2) + rows, f32),
            pltpu.VMEM((tile_cols, tile_cols), f32),
            pltpu.VMEM((STEPS, nests) + tile, f32),
            pltpu.VMEM((STEPS, 2) + tile, f32),
            dma,
            dma,
            dma((2, 2)),
            dma((2, nests)),
            dma((STEPS, 2)),
            dma((STEPS, 2)),
            dma((STEPS,)),
            dma((STEPS,)),
            dma((STEPS, nests)),
            dma((STEPS, 2)),
            dma((STEPS, nests)),
            dma((STEPS, 2)),
        ],
        compiler_params=pltpu.CompilerParams(
            collective_id=0, has_side_effects=True, vmem_limit_bytes=40 * 2**20
        ),
        cost_estimate=pl.CostEstimate(
            flops=20 * model_state.size, bytes_accessed=8 * model_state.size, transcendentals=0
        ),
    )(*arrays)


def solution(mesh):
    placed = (
        P("parts", "nest", "tx"),
        P(("parts", "nest"), "tx"),
        P("nest", "tx"),
        P("nest", "tx"),
        P("nest", None),
        P("nest", None),
        P("nest", "tx"),
        P(),
    )
    return jax.shard_map(
        functools.partial(per_device, dict(mesh.shape)),
        mesh=mesh,
        in_specs=placed,
        out_specs=P("parts", "nest", "tx"),
        check_vma=False,
    )
```

```python
import functools

import jax
import jax.numpy as jnp
from jax import lax
from jax.experimental import pallas as pl
from jax.experimental.pallas import tpu as pltpu
from jax.sharding import PartitionSpec as P

STEPS = 2
CHUNK = 8
BATCH = 4
PICK = 16
MESH = pl.DeviceIdType.MESH


def kernel(
    blocks,
    columns,
    state_hbm,
    diff_hbm,
    rim_index_hbm,
    rim_weight_hbm,
    side_index_hbm,
    side_weight_hbm,
    tile_ref,
    offset_ref,
    out_hbm,
    u0,
    u1,
    u2,
    diff_ref,
    rim_index_ref,
    rim_weight_ref,
    side_index_ref,
    side_weight_ref,
    idx_send,
    w_send,
    idx_recv,
    w_recv,
    row_weights,
    column_picks,
    col_send,
    col_recv,
    halo,
    row_send,
    row_recv,
    outer,
    rim_out,
    rim_recv,
    side_rows,
    side_out,
    side_recv,
    load_sem,
    small_sem,
    store_sem,
    param_send_sem,
    param_recv_sem,
    col_send_sem,
    col_recv_sem,
    row_send_sem,
    row_recv_sem,
    rim_send_sem,
    rim_recv_sem,
    side_send_sem,
    side_recv_sem,
):
    var_count, tile_rows, tile_cols = u0.shape
    groups = tile_rows // 8
    nests = blocks - 2
    me = lax.axis_index("nest")
    t = lax.axis_index("tx")
    right, left = lax.rem(t + 1, columns), lax.rem(t + columns - 1, columns)
    parity = lax.rem(me, 2)
    mate = me + 1 - 2 * parity
    is_parent = me < 2
    is_nest = me >= 2
    at_edge = jnp.logical_or(t == 0, t == columns - 1)

    smalls = [
        pltpu.make_async_copy(source, target, small_sem.at[i])
        for i, (source, target) in enumerate(
            (
                (rim_index_hbm, rim_index_ref),
                (rim_weight_hbm, rim_weight_ref),
                (side_index_hbm, side_index_ref),
                (side_weight_hbm, side_weight_ref),
                (diff_hbm, diff_ref),
            )
        )
    ]
    for copy in smalls:
        copy.start()
    loads = [
        pltpu.make_async_copy(
            state_hbm.at[pl.ds(i * CHUNK, CHUNK)], u0.at[pl.ds(i * CHUNK, CHUNK)], load_sem.at[i]
        )
        for i in range(var_count // CHUNK)
    ]
    for copy in loads:
        copy.start()

    barrier = pltpu.get_barrier_semaphore()
    pl.semaphore_signal(barrier, inc=1, device_id={"tx": left}, device_id_type=MESH)
    pl.semaphore_signal(barrier, inc=1, device_id={"tx": right}, device_id_type=MESH)
    pl.semaphore_signal(barrier, inc=1, device_id={"nest": mate}, device_id_type=MESH)

    @pl.when(is_nest)
    def _():
        for p in range(2):
            pl.semaphore_signal(barrier, inc=1, device_id={"nest": p}, device_id_type=MESH)
        pl.semaphore_wait(barrier, 5)

    @pl.when(is_parent)
    def _():
        for b in range(nests):
            pl.semaphore_signal(barrier, inc=1, device_id={"nest": 2 + b}, device_id_type=MESH)
        pl.semaphore_wait(barrier, 3 + nests)

    row_id = lax.broadcasted_iota(jnp.int32, (tile_rows, tile_cols), 0)
    lane = lax.broadcasted_iota(jnp.int32, (tile_rows, tile_cols), 1)
    lane8 = lax.broadcasted_iota(jnp.int32, (8, tile_cols), 1)
    half = tile_rows

    def param_copies(p, slot):
        return (
            pltpu.make_async_remote_copy(
                src_ref=idx_send,
                dst_ref=idx_recv.at[slot],
                send_sem=param_send_sem.at[0, p],
                recv_sem=param_recv_sem.at[0, slot],
                device_id={"nest": p},
                device_id_type=MESH,
            ),
            pltpu.make_async_remote_copy(
                src_ref=w_send.at[p],
                dst_ref=w_recv.at[slot],
                send_sem=param_send_sem.at[1, p],
                recv_sem=param_recv_sem.at[1, slot],
                device_id={"nest": p},
                device_id_type=MESH,
            ),
        )

    for copy in smalls:
        copy.wait()

    @pl.when(is_nest)
    def _():
        offset = offset_ref[me // 2]
        tile = tile_ref[0, 0]
        stay = (t == 0) == (parity == 0)
        index = side_index_ref[...]
        weight = side_weight_ref[...]
        turned_index = jnp.concatenate([index[:, half:], index[:, :half]], axis=1)
        turned_weight = jnp.concatenate([weight[:, half:], weight[:, :half]], axis=1)
        idx_send[0:4] = rim_index_ref[...] + offset
        idx_send[4:8] = jnp.where(stay, index, turned_index) + offset
        for p in range(2):
            keep = jnp.where(tile == p, 1.0, 0.0)
            w_send[p, 0:4] = rim_weight_ref[...] * keep
            w_send[p, 4:8] = jnp.where(stay, weight, turned_weight) * keep
        for p in range(2):
            for copy in param_copies(p, me - 2):
                copy.start()

    def col_copies(step):
        return (
            pltpu.make_async_remote_copy(
                src_ref=col_send.at[step],
                dst_ref=col_recv.at[step, 0],
                send_sem=col_send_sem.at[step, 0],
                recv_sem=col_recv_sem.at[step, 0],
                device_id={"tx": right},
                device_id_type=MESH,
            ),
            pltpu.make_async_remote_copy(
                src_ref=col_send.at[step],
                dst_ref=col_recv.at[step, 1],
                send_sem=col_send_sem.at[step, 1],
                recv_sem=col_recv_sem.at[step, 1],
                device_id={"tx": left},
                device_id_type=MESH,
            ),
            pltpu.make_async_remote_copy(
                src_ref=row_send.at[step],
                dst_ref=row_recv.at[step],
                send_sem=row_send_sem.at[step],
                recv_sem=row_recv_sem.at[step],
                device_id={"nest": mate},
                device_id_type=MESH,
            ),
        )

    def take_edges(step, v, tile):
        last, first = tile[tile_rows - 1 :], tile[:1]
        row_send[step, pl.ds(v, 1), :] = jnp.where(parity == 0, last, first)
        outer[pl.ds(v, 1), :] = jnp.where(parity == 0, first, last)
        col_send[step] = jnp.where(lane // 2 == v, pltpu.roll(tile, 2 * v + 1, 1), col_send[step])

    col_send[...] = jnp.zeros_like(col_send)
    for i, copy in enumerate(loads):
        copy.wait()

        def first_edges(trip, carry):
            for j in range(BATCH):
                v = i * CHUNK + trip * BATCH + j
                take_edges(0, v, u0[v])
            return carry

        lax.fori_loop(0, CHUNK // BATCH, first_edges, 0)
    for copy in col_copies(0):
        copy.start()

    def rim_copies(step, slot, p):
        return pltpu.make_async_remote_copy(
            src_ref=rim_out.at[step, slot],
            dst_ref=rim_recv.at[step, p],
            send_sem=rim_send_sem.at[step, slot],
            recv_sem=rim_recv_sem.at[step, p],
            device_id={"nest": 2 + slot},
            device_id_type=MESH,
        )

    def side_copies(step, slot, p):
        return pltpu.make_async_remote_copy(
            src_ref=side_out.at[step, slot],
            dst_ref=side_recv.at[step, p],
            send_sem=side_send_sem.at[step, slot],
            recv_sem=side_recv_sem.at[step, p],
            device_id={"nest": 2 + slot},
            device_id_type=MESH,
        )

    square = lax.broadcasted_iota(jnp.int32, (tile_cols, tile_cols), 0)

    def weights_of(index, weight):
        return jnp.where(row_id == index // tile_cols, weight, 0.0)

    def side_rows_of(pair):
        low = lane8[:4] < half
        index = jnp.where(low, idx_recv[2 * pair, 4:8], idx_recv[2 * pair + 1, 4:8])
        weight = jnp.where(low, w_recv[2 * pair, 4:8], w_recv[2 * pair + 1, 4:8])
        return index, weight

    def sets_of(pair, what):
        if what == 2:
            return side_rows_of(pair)
        return idx_recv[2 * pair + what, 0:4], w_recv[2 * pair + what, 0:4]

    def prepare():
        for slot in range(nests):
            for p in range(2):
                @pl.when(me == p)
                def _():
                    for copy in param_copies(p, slot):
                        copy.wait_recv()
        for pair in range(nests // 2):
            for what in range(3):
                index, weight = sets_of(pair, what)
                for k in range(4):
                    row_weights[pair, what, k] = weights_of(index[k : k + 1], weight[k : k + 1])
                    pick = jnp.where(square == lax.rem(index[k : k + 1], tile_cols), 1.0, 0.0).astype(jnp.bfloat16)
                    for part in range(2):
                        column_picks[
                            pair, what, part * tile_cols : (part + 1) * tile_cols, k * tile_cols : (k + 1) * tile_cols
                        ] = pick

    def interpolate(step, source):
        for pair in range(nests // 2):

            def run(whats):
                def one(trip, carry):
                    these = pl.ds(trip * PICK, PICK)
                    cells = source[these].reshape(PICK * tile_rows, tile_cols)
                    high = cells.astype(jnp.bfloat16)
                    low = (cells - high.astype(jnp.float32)).astype(jnp.bfloat16)
                    parts = jnp.concatenate([high, low], axis=1)
                    for what in whats:
                        total = jnp.zeros((PICK, 8, tile_cols), jnp.float32)
                        for two in range(2):
                            span = slice(2 * two * tile_cols, 2 * (two + 1) * tile_cols)
                            picked = jnp.dot(
                                parts, column_picks[pair, what, :, span], preferred_element_type=jnp.float32
                            )
                            for k in range(2):
                                one_k = picked[:, k * tile_cols : (k + 1) * tile_cols]
                                weighted = one_k.reshape(PICK, groups, 8, tile_cols) * row_weights[
                                    pair, what, 2 * two + k
                                ].reshape(1, groups, 8, tile_cols)
                                total = total + jnp.sum(weighted, axis=1)
                        value = jnp.sum(total, axis=1)
                        if what == 2:
                            side_rows[these, :] = value
                        else:
                            rim_out[step, 2 * pair + what, these, :] = value
                    return carry

                lax.fori_loop(0, var_count // PICK, one, 0)

            @pl.when(at_edge)
            def _():
                run((0, 1, 2))
                turned = side_rows[...].T
                for what in range(2):
                    side_out[step, 2 * pair + what] = jnp.take_along_axis(
                        turned[what * half : (what + 1) * half], lane // 2, axis=1, mode="promise_in_bounds"
                    )
                for what in range(2):
                    for p in range(2):
                        @pl.when(me == p)
                        def _():
                            side_copies(step, 2 * pair + what, p).start()

            @pl.when(jnp.logical_not(at_edge))
            def _():
                run((0, 1))

            for what in range(2):
                for p in range(2):
                    @pl.when(me == p)
                    def _():
                        rim_copies(step, 2 * pair + what, p).start()

    @pl.when(is_parent)
    def _():
        side_rows[...] = jnp.zeros_like(side_rows)
        prepare()
        interpolate(0, u0)

    def store(chunk):
        these = pl.ds(chunk * CHUNK, CHUNK)
        return pltpu.make_async_copy(u2.at[these], out_hbm.at[these], store_sem.at[chunk])

    for step in range(STEPS):
        source, target = ((u0, u1), (u1, u2))[step]
        to_right, to_left, to_mate = col_copies(step)
        to_right.wait_recv()
        to_left.wait_recv()
        to_mate.wait_recv()
        halo[...] = jnp.where(lane % 2 == 0, col_recv[step, 0], col_recv[step, 1])

        @pl.when(is_nest)
        def _():
            for p in range(2):
                rim_copies(step, 0, p).wait_recv()
            outer[...] = rim_recv[step, 0] + rim_recv[step, 1]

            @pl.when(at_edge)
            def _():
                for p in range(2):
                    side_copies(step, 0, p).wait_recv()
                own = lane % 2 == jnp.where(t == 0, 0, 1)
                halo[...] = jnp.where(own, side_recv[step, 0] + side_recv[step, 1], halo[...])

        def update(v):
            u = source[v]
            mate_row = row_recv[step, pl.ds(v, 1), :]
            outer_row = outer[pl.ds(v, 1), :]
            top = jnp.where(parity == 0, outer_row, mate_row)
            bottom = jnp.where(parity == 0, mate_row, outer_row)
            ghost = pltpu.roll(halo[...], tile_cols - 1 - 2 * v, 1)
            left_side = pltpu.roll(jnp.where(lane == tile_cols - 1, ghost, u), 1, 1)
            right_side = pltpu.roll(jnp.where(lane == 0, ghost, u), tile_cols - 1, 1)
            above = jnp.where(row_id == 0, top, pltpu.roll(u, 1, 0))
            below = jnp.where(row_id == tile_rows - 1, bottom, pltpu.roll(u, tile_rows - 1, 0))
            laplace = above + below + left_side + right_side - 4.0 * u
            new = u + diff_ref[...] * laplace
            target[v] = new
            if step + 1 < STEPS:
                take_edges(step + 1, v, new)

        def one(chunk, carry):
            def inner(trip, carry):
                for j in range(BATCH):
                    update(chunk * CHUNK + trip * BATCH + j)
                return carry

            lax.fori_loop(0, CHUNK // BATCH, inner, 0)
            if step == STEPS - 1:
                store(chunk).start()
            return carry

        lax.fori_loop(0, var_count // CHUNK, one, 0)
        if step + 1 < STEPS:
            for copy in col_copies(step + 1):
                copy.start()

            @pl.when(is_parent)
            def _():
                interpolate(step + 1, target)

    for step in range(STEPS):
        for copy in col_copies(step):
            copy.wait_send()

    @pl.when(is_nest)
    def _():
        for p in range(2):
            for copy in param_copies(p, 0):
                copy.wait_send()

    @pl.when(is_parent)
    def _():
        for step in range(STEPS):
            for slot in range(nests):
                rim_copies(step, slot, 0).wait_send()

                @pl.when(at_edge)
                def _():
                    side_copies(step, slot, 0).wait_send()

    for chunk in range(var_count // CHUNK):
        store(chunk).wait()


def per_device(mesh_shape, *arrays):
    model_state = arrays[0]
    var_count, tile_rows, tile_cols = model_state.shape
    blocks, columns = mesh_shape["nest"], mesh_shape["tx"]
    nests = blocks - 2
    f32 = jnp.float32
    tile = (tile_rows, tile_cols)
    rows = (var_count, tile_cols)
    smem = pl.BlockSpec(memory_space=pltpu.SMEM)
    hbm = pl.BlockSpec(memory_space=pltpu.HBM)
    dma = pltpu.SemaphoreType.DMA
    return pl.pallas_call(
        functools.partial(kernel, blocks, columns),
        out_shape=jax.ShapeDtypeStruct(model_state.shape, f32),
        in_specs=[hbm] * 6 + [smem] * 2,
        out_specs=hbm,
        scratch_shapes=[
            pltpu.VMEM(model_state.shape, f32),
            pltpu.VMEM(model_state.shape, f32),
            pltpu.VMEM(model_state.shape, f32),
            pltpu.VMEM(tile, f32),
            pltpu.VMEM((4, tile_cols), jnp.int32),
            pltpu.VMEM((4, tile_cols), f32),
            pltpu.VMEM((4, tile_cols), jnp.int32),
            pltpu.VMEM((4, tile_cols), f32),
            pltpu.VMEM((8, tile_cols), jnp.int32),
            pltpu.VMEM((2, 8, tile_cols), f32),
            pltpu.VMEM((nests, 8, tile_cols), jnp.int32),
            pltpu.VMEM((nests, 8, tile_cols), f32),
            pltpu.VMEM((nests // 2, 3, 4) + tile, f32),
            pltpu.VMEM((nests // 2, 3, 2 * tile_cols, 4 * tile_cols), jnp.bfloat16),
            pltpu.VMEM((STEPS,) + tile, f32),
            pltpu.VMEM((STEPS, 2) + tile, f32),
            pltpu.VMEM(tile, f32),
            pltpu.VMEM((STEPS,) + rows, f32),
            pltpu.VMEM((STEPS,) + rows, f32),
            pltpu.VMEM(rows, f32),
            pltpu.VMEM((STEPS, nests) + rows, f32),
            pltpu.VMEM((STEPS, 2) + rows, f32),
            pltpu.VMEM((tile_cols, tile_cols), f32),
            pltpu.VMEM((STEPS, nests) + tile, f32),
            pltpu.VMEM((STEPS, 2) + tile, f32),
            dma((var_count // CHUNK,)),
            dma((5,)),
            dma((var_count // CHUNK,)),
            dma((2, 2)),
            dma((2, nests)),
            dma((STEPS, 2)),
            dma((STEPS, 2)),
            dma((STEPS,)),
            dma((STEPS,)),
            dma((STEPS, nests)),
            dma((STEPS, 2)),
            dma((STEPS, nests)),
            dma((STEPS, 2)),
        ],
        compiler_params=pltpu.CompilerParams(
            collective_id=0, has_side_effects=True, vmem_limit_bytes=64 * 2**20
        ),
        cost_estimate=pl.CostEstimate(
            flops=20 * model_state.size, bytes_accessed=8 * model_state.size, transcendentals=0
        ),
    )(*arrays)


def solution(mesh):
    placed = (
        P("parts", "nest", "tx"),
        P(("parts", "nest"), "tx"),
        P("nest", "tx"),
        P("nest", "tx"),
        P("nest", None),
        P("nest", None),
        P("nest", "tx"),
        P(),
    )
    return jax.shard_map(
        functools.partial(per_device, dict(mesh.shape)),
        mesh=mesh,
        in_specs=placed,
        out_specs=P("parts", "nest", "tx"),
        check_vma=False,
    )
```

```python
import functools

import jax
import jax.numpy as jnp
from jax import lax
from jax.experimental import pallas as pl
from jax.experimental.pallas import tpu as pltpu
from jax.sharding import PartitionSpec as P

STEPS = 2
CHUNK = 8
BATCH = 8
PICK = 16
MESH = pl.DeviceIdType.MESH


def kernel(
    blocks,
    columns,
    state_hbm,
    diff_hbm,
    rim_index_hbm,
    rim_weight_hbm,
    side_index_hbm,
    side_weight_hbm,
    tile_ref,
    offset_ref,
    out_hbm,
    u0,
    u1,
    u2,
    diff_ref,
    rim_index_ref,
    rim_weight_ref,
    side_index_ref,
    side_weight_ref,
    idx_send,
    w_send,
    idx_recv,
    w_recv,
    row_weights,
    column_picks,
    beside,
    col_send,
    col_recv,
    halo,
    row_send,
    row_recv,
    outer,
    rim_out,
    rim_recv,
    side_rows,
    side_out,
    side_recv,
    load_sem,
    small_sem,
    store_sem,
    param_send_sem,
    param_recv_sem,
    col_send_sem,
    col_recv_sem,
    row_send_sem,
    row_recv_sem,
    rim_send_sem,
    rim_recv_sem,
    side_send_sem,
    side_recv_sem,
):
    var_count, tile_rows, tile_cols = u0.shape
    groups = tile_rows // 8
    nests = blocks - 2
    me = lax.axis_index("nest")
    t = lax.axis_index("tx")
    right, left = lax.rem(t + 1, columns), lax.rem(t + columns - 1, columns)
    parity = lax.rem(me, 2)
    mate = me + 1 - 2 * parity
    is_parent = me < 2
    is_nest = me >= 2
    at_edge = jnp.logical_or(t == 0, t == columns - 1)

    smalls = [
        pltpu.make_async_copy(source, target, small_sem.at[i])
        for i, (source, target) in enumerate(
            (
                (rim_index_hbm, rim_index_ref),
                (rim_weight_hbm, rim_weight_ref),
                (side_index_hbm, side_index_ref),
                (side_weight_hbm, side_weight_ref),
                (diff_hbm, diff_ref),
            )
        )
    ]
    for copy in smalls:
        copy.start()
    loads = [
        pltpu.make_async_copy(
            state_hbm.at[pl.ds(i * CHUNK, CHUNK)], u0.at[pl.ds(i * CHUNK, CHUNK)], load_sem.at[i]
        )
        for i in range(var_count // CHUNK)
    ]
    for copy in loads:
        copy.start()

    barrier = pltpu.get_barrier_semaphore()
    pl.semaphore_signal(barrier, inc=1, device_id={"tx": left}, device_id_type=MESH)
    pl.semaphore_signal(barrier, inc=1, device_id={"tx": right}, device_id_type=MESH)
    pl.semaphore_signal(barrier, inc=1, device_id={"nest": mate}, device_id_type=MESH)

    @pl.when(is_nest)
    def _():
        for p in range(2):
            pl.semaphore_signal(barrier, inc=1, device_id={"nest": p}, device_id_type=MESH)
        pl.semaphore_wait(barrier, 5)

    @pl.when(is_parent)
    def _():
        for b in range(nests):
            pl.semaphore_signal(barrier, inc=1, device_id={"nest": 2 + b}, device_id_type=MESH)
        pl.semaphore_wait(barrier, 3 + nests)

    row_id = lax.broadcasted_iota(jnp.int32, (tile_rows, tile_cols), 0)
    lane = lax.broadcasted_iota(jnp.int32, (tile_rows, tile_cols), 1)
    lane8 = lax.broadcasted_iota(jnp.int32, (8, tile_cols), 1)
    half = tile_rows

    def param_copies(p, slot):
        return (
            pltpu.make_async_remote_copy(
                src_ref=idx_send,
                dst_ref=idx_recv.at[slot],
                send_sem=param_send_sem.at[0, p],
                recv_sem=param_recv_sem.at[0, slot],
                device_id={"nest": p},
                device_id_type=MESH,
            ),
            pltpu.make_async_remote_copy(
                src_ref=w_send.at[p],
                dst_ref=w_recv.at[slot],
                send_sem=param_send_sem.at[1, p],
                recv_sem=param_recv_sem.at[1, slot],
                device_id={"nest": p},
                device_id_type=MESH,
            ),
        )

    for copy in smalls:
        copy.wait()

    @pl.when(is_nest)
    def _():
        offset = offset_ref[me // 2]
        tile = tile_ref[0, 0]
        stay = (t == 0) == (parity == 0)
        index = side_index_ref[...]
        weight = side_weight_ref[...]
        turned_index = jnp.concatenate([index[:, half:], index[:, :half]], axis=1)
        turned_weight = jnp.concatenate([weight[:, half:], weight[:, :half]], axis=1)
        idx_send[0:4] = rim_index_ref[...] + offset
        idx_send[4:8] = jnp.where(stay, index, turned_index) + offset
        for p in range(2):
            keep = jnp.where(tile == p, 1.0, 0.0)
            w_send[p, 0:4] = rim_weight_ref[...] * keep
            w_send[p, 4:8] = jnp.where(stay, weight, turned_weight) * keep
        for p in range(2):
            for copy in param_copies(p, me - 2):
                copy.start()

    def col_copies(step):
        return (
            pltpu.make_async_remote_copy(
                src_ref=col_send.at[step],
                dst_ref=col_recv.at[step, 0],
                send_sem=col_send_sem.at[step, 0],
                recv_sem=col_recv_sem.at[step, 0],
                device_id={"tx": right},
                device_id_type=MESH,
            ),
            pltpu.make_async_remote_copy(
                src_ref=col_send.at[step],
                dst_ref=col_recv.at[step, 1],
                send_sem=col_send_sem.at[step, 1],
                recv_sem=col_recv_sem.at[step, 1],
                device_id={"tx": left},
                device_id_type=MESH,
            ),
            pltpu.make_async_remote_copy(
                src_ref=row_send.at[step],
                dst_ref=row_recv.at[step],
                send_sem=row_send_sem.at[step],
                recv_sem=row_recv_sem.at[step],
                device_id={"nest": mate},
                device_id_type=MESH,
            ),
        )

    def take_edges(step, v, tile):
        last, first = tile[tile_rows - 1 :], tile[:1]
        row_send[step, pl.ds(v, 1), :] = jnp.where(parity == 0, last, first)
        outer[pl.ds(v, 1), :] = jnp.where(parity == 0, first, last)
        col_send[step] = jnp.where(lane // 2 == v, pltpu.roll(tile, 2 * v + 1, 1), col_send[step])

    col_send[...] = jnp.zeros_like(col_send)
    for i, copy in enumerate(loads):
        copy.wait()

        def first_edges(trip, carry):
            for j in range(BATCH):
                v = i * CHUNK + trip * BATCH + j
                take_edges(0, v, u0[v])
            return carry

        lax.fori_loop(0, CHUNK // BATCH, first_edges, 0)
    for copy in col_copies(0):
        copy.start()

    def rim_copies(step, slot, p):
        return pltpu.make_async_remote_copy(
            src_ref=rim_out.at[step, slot],
            dst_ref=rim_recv.at[step, p],
            send_sem=rim_send_sem.at[step, slot],
            recv_sem=rim_recv_sem.at[step, p],
            device_id={"nest": 2 + slot},
            device_id_type=MESH,
        )

    def side_copies(step, slot, p):
        return pltpu.make_async_remote_copy(
            src_ref=side_out.at[step, slot],
            dst_ref=side_recv.at[step, p],
            send_sem=side_send_sem.at[step, slot],
            recv_sem=side_recv_sem.at[step, p],
            device_id={"nest": 2 + slot},
            device_id_type=MESH,
        )

    def split(cells):
        high = cells.astype(jnp.bfloat16)
        low = (cells - high.astype(jnp.float32)).astype(jnp.bfloat16)
        return jnp.concatenate([high, low], axis=1)

    square = lax.broadcasted_iota(jnp.int32, (tile_cols, tile_cols), 0)

    def weights_of(index, weight):
        return jnp.where(row_id == index // tile_cols, weight, 0.0)

    def side_rows_of(pair):
        low = lane8[:4] < half
        index = jnp.where(low, idx_recv[2 * pair, 4:8], idx_recv[2 * pair + 1, 4:8])
        weight = jnp.where(low, w_recv[2 * pair, 4:8], w_recv[2 * pair + 1, 4:8])
        return index, weight

    def sets_of(pair, what):
        if what == 2:
            return side_rows_of(pair)
        return idx_recv[2 * pair + what, 0:4], w_recv[2 * pair + what, 0:4]

    def prepare():
        for slot in range(nests):
            for p in range(2):
                @pl.when(me == p)
                def _():
                    for copy in param_copies(p, slot):
                        copy.wait_recv()
        for pair in range(nests // 2):
            for what in range(3):
                index, weight = sets_of(pair, what)
                for k in range(4):
                    row_weights[pair, what, k] = weights_of(index[k : k + 1], weight[k : k + 1])
                    pick = jnp.where(square == lax.rem(index[k : k + 1], tile_cols), 1.0, 0.0).astype(jnp.bfloat16)
                    for part in range(2):
                        column_picks[
                            pair, what, part * tile_cols : (part + 1) * tile_cols, k * tile_cols : (k + 1) * tile_cols
                        ] = pick

    def interpolate(step, source):
        for pair in range(nests // 2):

            def run(whats):
                def one(trip, carry):
                    these = pl.ds(trip * PICK, PICK)
                    parts = split(source[these].reshape(PICK * tile_rows, tile_cols))
                    for what in whats:
                        total = jnp.zeros((PICK, 8, tile_cols), jnp.float32)
                        for two in range(2):
                            span = slice(2 * two * tile_cols, 2 * (two + 1) * tile_cols)
                            picked = jnp.dot(
                                parts, column_picks[pair, what, :, span], preferred_element_type=jnp.float32
                            )
                            for k in range(2):
                                one_k = picked[:, k * tile_cols : (k + 1) * tile_cols]
                                weighted = one_k.reshape(PICK, groups, 8, tile_cols) * row_weights[
                                    pair, what, 2 * two + k
                                ].reshape(1, groups, 8, tile_cols)
                                total = total + jnp.sum(weighted, axis=1)
                        value = jnp.sum(total, axis=1)
                        if what == 2:
                            side_rows[these, :] = value
                        else:
                            rim_out[step, 2 * pair + what, these, :] = value
                    return carry

                lax.fori_loop(0, var_count // PICK, one, 0)

            @pl.when(at_edge)
            def _():
                run((0, 1, 2))
                turned = side_rows[...].T
                for what in range(2):
                    side_out[step, 2 * pair + what] = jnp.take_along_axis(
                        turned[what * half : (what + 1) * half], lane // 2, axis=1, mode="promise_in_bounds"
                    )
                for what in range(2):
                    for p in range(2):
                        @pl.when(me == p)
                        def _():
                            side_copies(step, 2 * pair + what, p).start()

            @pl.when(jnp.logical_not(at_edge))
            def _():
                run((0, 1))

            for what in range(2):
                for p in range(2):
                    @pl.when(me == p)
                    def _():
                        rim_copies(step, 2 * pair + what, p).start()

    distance = square - lax.broadcasted_iota(jnp.int32, (tile_cols, tile_cols), 1)
    neighbours = jnp.where((distance == 1) | (distance == -1), 1.0, 0.0).astype(jnp.bfloat16)
    for part in range(2):
        beside[part * tile_cols : (part + 1) * tile_cols] = neighbours

    @pl.when(is_parent)
    def _():
        side_rows[...] = jnp.zeros_like(side_rows)
        prepare()
        interpolate(0, u0)

    def store(chunk):
        these = pl.ds(chunk * BATCH, BATCH)
        return pltpu.make_async_copy(u2.at[these], out_hbm.at[these], store_sem.at[chunk])

    for step in range(STEPS):
        source, target = ((u0, u1), (u1, u2))[step]
        to_right, to_left, to_mate = col_copies(step)
        to_right.wait_recv()
        to_left.wait_recv()
        to_mate.wait_recv()
        halo[...] = jnp.where(
            lane % 2 == 0,
            pltpu.roll(col_recv[step, 1], tile_cols - 1, 1),
            pltpu.roll(col_recv[step, 0], 1, 1),
        )

        @pl.when(is_nest)
        def _():
            for p in range(2):
                rim_copies(step, 0, p).wait_recv()
            outer[...] = rim_recv[step, 0] + rim_recv[step, 1]

            @pl.when(at_edge)
            def _():
                for p in range(2):
                    side_copies(step, 0, p).wait_recv()
                own = lane % 2 == jnp.where(t == 0, 1, 0)
                halo[...] = jnp.where(own, side_recv[step, 0] + side_recv[step, 1], halo[...])

        def update(v, u, sides):
            mate_row = row_recv[step, pl.ds(v, 1), :]
            outer_row = outer[pl.ds(v, 1), :]
            top = jnp.where(parity == 0, outer_row, mate_row)
            bottom = jnp.where(parity == 0, mate_row, outer_row)
            ghost = pltpu.roll(halo[...], tile_cols - 1 - 2 * v, 1)
            sides = sides + jnp.where((lane == 0) | (lane == tile_cols - 1), ghost, 0.0)
            above = jnp.where(row_id == 0, top, pltpu.roll(u, 1, 0))
            below = jnp.where(row_id == tile_rows - 1, bottom, pltpu.roll(u, tile_rows - 1, 0))
            laplace = above + below + sides - 4.0 * u
            new = u + diff_ref[...] * laplace
            target[v] = new
            if step + 1 < STEPS:
                take_edges(step + 1, v, new)

        def one(chunk, carry):
            cells = source[pl.ds(chunk * BATCH, BATCH)]
            sides = jnp.dot(
                split(cells.reshape(BATCH * tile_rows, tile_cols)), beside[...], preferred_element_type=jnp.float32
            )
            for j in range(BATCH):
                update(chunk * BATCH + j, cells[j], sides[j * tile_rows : (j + 1) * tile_rows])
            if step == STEPS - 1:
                store(chunk).start()
            return carry

        lax.fori_loop(0, var_count // BATCH, one, 0)
        if step + 1 < STEPS:
            for copy in col_copies(step + 1):
                copy.start()

            @pl.when(is_parent)
            def _():
                interpolate(step + 1, target)

    for step in range(STEPS):
        for copy in col_copies(step):
            copy.wait_send()

    @pl.when(is_nest)
    def _():
        for p in range(2):
            for copy in param_copies(p, 0):
                copy.wait_send()

    @pl.when(is_parent)
    def _():
        for step in range(STEPS):
            for slot in range(nests):
                rim_copies(step, slot, 0).wait_send()

                @pl.when(at_edge)
                def _():
                    side_copies(step, slot, 0).wait_send()

    for chunk in range(var_count // BATCH):
        store(chunk).wait()


def per_device(mesh_shape, *arrays):
    model_state = arrays[0]
    var_count, tile_rows, tile_cols = model_state.shape
    blocks, columns = mesh_shape["nest"], mesh_shape["tx"]
    nests = blocks - 2
    f32 = jnp.float32
    tile = (tile_rows, tile_cols)
    rows = (var_count, tile_cols)
    smem = pl.BlockSpec(memory_space=pltpu.SMEM)
    hbm = pl.BlockSpec(memory_space=pltpu.HBM)
    dma = pltpu.SemaphoreType.DMA
    return pl.pallas_call(
        functools.partial(kernel, blocks, columns),
        out_shape=jax.ShapeDtypeStruct(model_state.shape, f32),
        in_specs=[hbm] * 6 + [smem] * 2,
        out_specs=hbm,
        scratch_shapes=[
            pltpu.VMEM(model_state.shape, f32),
            pltpu.VMEM(model_state.shape, f32),
            pltpu.VMEM(model_state.shape, f32),
            pltpu.VMEM(tile, f32),
            pltpu.VMEM((4, tile_cols), jnp.int32),
            pltpu.VMEM((4, tile_cols), f32),
            pltpu.VMEM((4, tile_cols), jnp.int32),
            pltpu.VMEM((4, tile_cols), f32),
            pltpu.VMEM((8, tile_cols), jnp.int32),
            pltpu.VMEM((2, 8, tile_cols), f32),
            pltpu.VMEM((nests, 8, tile_cols), jnp.int32),
            pltpu.VMEM((nests, 8, tile_cols), f32),
            pltpu.VMEM((nests // 2, 3, 4) + tile, f32),
            pltpu.VMEM((nests // 2, 3, 2 * tile_cols, 4 * tile_cols), jnp.bfloat16),
            pltpu.VMEM((2 * tile_cols, tile_cols), jnp.bfloat16),
            pltpu.VMEM((STEPS,) + tile, f32),
            pltpu.VMEM((STEPS, 2) + tile, f32),
            pltpu.VMEM(tile, f32),
            pltpu.VMEM((STEPS,) + rows, f32),
            pltpu.VMEM((STEPS,) + rows, f32),
            pltpu.VMEM(rows, f32),
            pltpu.VMEM((STEPS, nests) + rows, f32),
            pltpu.VMEM((STEPS, 2) + rows, f32),
            pltpu.VMEM((tile_cols, tile_cols), f32),
            pltpu.VMEM((STEPS, nests) + tile, f32),
            pltpu.VMEM((STEPS, 2) + tile, f32),
            dma((var_count // CHUNK,)),
            dma((5,)),
            dma((var_count // BATCH,)),
            dma((2, 2)),
            dma((2, nests)),
            dma((STEPS, 2)),
            dma((STEPS, 2)),
            dma((STEPS,)),
            dma((STEPS,)),
            dma((STEPS, nests)),
            dma((STEPS, 2)),
            dma((STEPS, nests)),
            dma((STEPS, 2)),
        ],
        compiler_params=pltpu.CompilerParams(
            collective_id=0, has_side_effects=True, vmem_limit_bytes=64 * 2**20
        ),
        cost_estimate=pl.CostEstimate(
            flops=20 * model_state.size, bytes_accessed=8 * model_state.size, transcendentals=0
        ),
    )(*arrays)


def solution(mesh):
    placed = (
        P("parts", "nest", "tx"),
        P(("parts", "nest"), "tx"),
        P("nest", "tx"),
        P("nest", "tx"),
        P("nest", None),
        P("nest", None),
        P("nest", "tx"),
        P(),
    )
    return jax.shard_map(
        functools.partial(per_device, dict(mesh.shape)),
        mesh=mesh,
        in_specs=placed,
        out_specs=P("parts", "nest", "tx"),
        check_vma=False,
    )
```

```python
import functools

import jax
import jax.numpy as jnp
from jax import lax
from jax.experimental import pallas as pl
from jax.experimental.pallas import tpu as pltpu
from jax.sharding import PartitionSpec as P

STEPS = 2
CHUNK = 8
BATCH = 8
PICK = 16
MESH = pl.DeviceIdType.MESH


def kernel(
    blocks,
    columns,
    state_hbm,
    diff_hbm,
    rim_index_hbm,
    rim_weight_hbm,
    side_index_hbm,
    side_weight_hbm,
    tile_ref,
    offset_ref,
    out_hbm,
    u0,
    u1,
    u2,
    diff_ref,
    rim_index_ref,
    rim_weight_ref,
    side_index_ref,
    side_weight_ref,
    idx_send,
    w_send,
    idx_recv,
    w_recv,
    row_weights,
    column_picks,
    beside,
    col_send,
    col_recv,
    halo,
    row_send,
    row_recv,
    outer,
    rim_out,
    rim_recv,
    side_rows,
    side_out,
    side_recv,
    load_sem,
    small_sem,
    store_sem,
    param_send_sem,
    param_recv_sem,
    col_send_sem,
    col_recv_sem,
    row_send_sem,
    row_recv_sem,
    rim_send_sem,
    rim_recv_sem,
    side_send_sem,
    side_recv_sem,
):
    var_count, tile_rows, tile_cols = u0.shape
    groups = tile_rows // 8
    nests = blocks - 2
    me = lax.axis_index("nest")
    t = lax.axis_index("tx")
    right, left = lax.rem(t + 1, columns), lax.rem(t + columns - 1, columns)
    parity = lax.rem(me, 2)
    mate = me + 1 - 2 * parity
    is_parent = me < 2
    is_nest = me >= 2
    at_edge = jnp.logical_or(t == 0, t == columns - 1)

    smalls = [
        pltpu.make_async_copy(source, target, small_sem.at[i])
        for i, (source, target) in enumerate(
            (
                (rim_index_hbm, rim_index_ref),
                (rim_weight_hbm, rim_weight_ref),
                (side_index_hbm, side_index_ref),
                (side_weight_hbm, side_weight_ref),
                (diff_hbm, diff_ref),
            )
        )
    ]
    for copy in smalls:
        copy.start()
    loads = [
        pltpu.make_async_copy(
            state_hbm.at[pl.ds(i * CHUNK, CHUNK)], u0.at[pl.ds(i * CHUNK, CHUNK)], load_sem.at[i]
        )
        for i in range(var_count // CHUNK)
    ]
    for copy in loads:
        copy.start()

    barrier = pltpu.get_barrier_semaphore()
    pl.semaphore_signal(barrier, inc=1, device_id={"tx": left}, device_id_type=MESH)
    pl.semaphore_signal(barrier, inc=1, device_id={"tx": right}, device_id_type=MESH)
    pl.semaphore_signal(barrier, inc=1, device_id={"nest": mate}, device_id_type=MESH)

    @pl.when(is_nest)
    def _():
        for p in range(2):
            pl.semaphore_signal(barrier, inc=1, device_id={"nest": p}, device_id_type=MESH)
        pl.semaphore_wait(barrier, 5)

    @pl.when(is_parent)
    def _():
        for b in range(nests):
            pl.semaphore_signal(barrier, inc=1, device_id={"nest": 2 + b}, device_id_type=MESH)
        pl.semaphore_wait(barrier, 3 + nests)

    row_id = lax.broadcasted_iota(jnp.int32, (tile_rows, tile_cols), 0)
    lane = lax.broadcasted_iota(jnp.int32, (tile_rows, tile_cols), 1)
    lane8 = lax.broadcasted_iota(jnp.int32, (8, tile_cols), 1)
    half = tile_rows

    def param_copies(p, slot):
        return (
            pltpu.make_async_remote_copy(
                src_ref=idx_send,
                dst_ref=idx_recv.at[slot],
                send_sem=param_send_sem.at[0, p],
                recv_sem=param_recv_sem.at[0, slot],
                device_id={"nest": p},
                device_id_type=MESH,
            ),
            pltpu.make_async_remote_copy(
                src_ref=w_send.at[p],
                dst_ref=w_recv.at[slot],
                send_sem=param_send_sem.at[1, p],
                recv_sem=param_recv_sem.at[1, slot],
                device_id={"nest": p},
                device_id_type=MESH,
            ),
        )

    for copy in smalls:
        copy.wait()

    @pl.when(is_nest)
    def _():
        offset = offset_ref[me // 2]
        tile = tile_ref[0, 0]
        stay = (t == 0) == (parity == 0)
        index = side_index_ref[...]
        weight = side_weight_ref[...]
        turned_index = jnp.concatenate([index[:, half:], index[:, :half]], axis=1)
        turned_weight = jnp.concatenate([weight[:, half:], weight[:, :half]], axis=1)
        idx_send[0:4] = rim_index_ref[...] + offset
        idx_send[4:8] = jnp.where(stay, index, turned_index) + offset
        for p in range(2):
            keep = jnp.where(tile == p, 1.0, 0.0)
            w_send[p, 0:4] = rim_weight_ref[...] * keep
            w_send[p, 4:8] = jnp.where(stay, weight, turned_weight) * keep
        for p in range(2):
            for copy in param_copies(p, me - 2):
                copy.start()

    def col_copies(step):
        return (
            pltpu.make_async_remote_copy(
                src_ref=col_send.at[step],
                dst_ref=col_recv.at[step, 0],
                send_sem=col_send_sem.at[step, 0],
                recv_sem=col_recv_sem.at[step, 0],
                device_id={"tx": right},
                device_id_type=MESH,
            ),
            pltpu.make_async_remote_copy(
                src_ref=col_send.at[step],
                dst_ref=col_recv.at[step, 1],
                send_sem=col_send_sem.at[step, 1],
                recv_sem=col_recv_sem.at[step, 1],
                device_id={"tx": left},
                device_id_type=MESH,
            ),
            pltpu.make_async_remote_copy(
                src_ref=row_send.at[step],
                dst_ref=row_recv.at[step],
                send_sem=row_send_sem.at[step],
                recv_sem=row_recv_sem.at[step],
                device_id={"nest": mate},
                device_id_type=MESH,
            ),
        )

    def take_edges(step, v, tile):
        last, first = tile[tile_rows - 1 :], tile[:1]
        row_send[step, pl.ds(v, 1), :] = jnp.where(parity == 0, last, first)
        outer[pl.ds(v, 1), :] = jnp.where(parity == 0, first, last)
        col_send[step] = jnp.where(lane // 2 == v, pltpu.roll(tile, 2 * v + 1, 1), col_send[step])

    col_send[...] = jnp.zeros_like(col_send)
    for i, copy in enumerate(loads):
        copy.wait()

        def first_edges(trip, carry):
            for j in range(BATCH):
                v = i * CHUNK + trip * BATCH + j
                take_edges(0, v, u0[v])
            return carry

        lax.fori_loop(0, CHUNK // BATCH, first_edges, 0)
    for copy in col_copies(0):
        copy.start()

    def rim_copies(step, slot, p):
        return pltpu.make_async_remote_copy(
            src_ref=rim_out.at[step, slot],
            dst_ref=rim_recv.at[step, p],
            send_sem=rim_send_sem.at[step, slot],
            recv_sem=rim_recv_sem.at[step, p],
            device_id={"nest": 2 + slot},
            device_id_type=MESH,
        )

    def side_copies(step, slot, p):
        return pltpu.make_async_remote_copy(
            src_ref=side_out.at[step, slot],
            dst_ref=side_recv.at[step, p],
            send_sem=side_send_sem.at[step, slot],
            recv_sem=side_recv_sem.at[step, p],
            device_id={"nest": 2 + slot},
            device_id_type=MESH,
        )

    def split(cells):
        high = cells.astype(jnp.bfloat16)
        low = (cells - high.astype(jnp.float32)).astype(jnp.bfloat16)
        return jnp.concatenate([high, low], axis=1)

    square = lax.broadcasted_iota(jnp.int32, (tile_cols, tile_cols), 0)

    def weights_of(index, weight):
        return jnp.where(row_id == index // tile_cols, weight, 0.0)

    def side_rows_of(pair):
        low = lane8[:4] < half
        index = jnp.where(low, idx_recv[2 * pair, 4:8], idx_recv[2 * pair + 1, 4:8])
        weight = jnp.where(low, w_recv[2 * pair, 4:8], w_recv[2 * pair + 1, 4:8])
        return index, weight

    def sets_of(pair, what):
        if what == 2:
            return side_rows_of(pair)
        return idx_recv[2 * pair + what, 0:4], w_recv[2 * pair + what, 0:4]

    def prepare():
        for slot in range(nests):
            for p in range(2):
                @pl.when(me == p)
                def _():
                    for copy in param_copies(p, slot):
                        copy.wait_recv()
        for pair in range(nests // 2):
            for what in range(3):
                index, weight = sets_of(pair, what)
                for k in range(4):
                    row_weights[pair, what, k] = weights_of(index[k : k + 1], weight[k : k + 1])
                    pick = jnp.where(square == lax.rem(index[k : k + 1], tile_cols), 1.0, 0.0).astype(jnp.bfloat16)
                    for part in range(2):
                        column_picks[
                            pair, what, part * tile_cols : (part + 1) * tile_cols, k * tile_cols : (k + 1) * tile_cols
                        ] = pick

    def interpolate(step, source):
        for pair in range(nests // 2):

            def run(whats):
                def one(trip, carry):
                    these = pl.ds(trip * PICK, PICK)
                    parts = split(source[these].reshape(PICK * tile_rows, tile_cols))
                    for what in whats:
                        total = jnp.zeros((PICK, 8, tile_cols), jnp.float32)
                        for two in range(2):
                            span = slice(2 * two * tile_cols, 2 * (two + 1) * tile_cols)
                            picked = jnp.dot(
                                parts, column_picks[pair, what, :, span], preferred_element_type=jnp.float32
                            )
                            for k in range(2):
                                one_k = picked[:, k * tile_cols : (k + 1) * tile_cols]
                                weighted = one_k.reshape(PICK, groups, 8, tile_cols) * row_weights[
                                    pair, what, 2 * two + k
                                ].reshape(1, groups, 8, tile_cols)
                                total = total + jnp.sum(weighted, axis=1)
                        value = jnp.sum(total, axis=1)
                        if what == 2:
                            side_rows[these, :] = value
                        else:
                            rim_out[step, 2 * pair + what, these, :] = value
                    return carry

                lax.fori_loop(0, var_count // PICK, one, 0)

            @pl.when(at_edge)
            def _():
                run((0, 1, 2))
                turned = side_rows[...].T
                for what in range(2):
                    side_out[step, 2 * pair + what] = jnp.take_along_axis(
                        turned[what * half : (what + 1) * half], lane // 2, axis=1, mode="promise_in_bounds"
                    )
                for what in range(2):
                    for p in range(2):
                        @pl.when(me == p)
                        def _():
                            side_copies(step, 2 * pair + what, p).start()

            @pl.when(jnp.logical_not(at_edge))
            def _():
                run((0, 1))

            for what in range(2):
                for p in range(2):
                    @pl.when(me == p)
                    def _():
                        rim_copies(step, 2 * pair + what, p).start()

    distance = square - lax.broadcasted_iota(jnp.int32, (tile_cols, tile_cols), 1)
    neighbours = jnp.where((distance == 1) | (distance == -1), 1.0, 0.0).astype(jnp.bfloat16)
    for part in range(2):
        beside[part * tile_cols : (part + 1) * tile_cols] = neighbours

    @pl.when(is_parent)
    def _():
        side_rows[...] = jnp.zeros_like(side_rows)
        prepare()
        interpolate(0, u0)

    def store(chunk):
        these = pl.ds(chunk * BATCH, BATCH)
        return pltpu.make_async_copy(u2.at[these], out_hbm.at[these], store_sem.at[chunk])

    for step in range(STEPS):
        source, target = ((u0, u1), (u1, u2))[step]
        to_right, to_left, to_mate = col_copies(step)
        to_right.wait_recv()
        to_left.wait_recv()
        to_mate.wait_recv()
        halo[...] = jnp.where(
            lane % 2 == 0,
            pltpu.roll(col_recv[step, 1], tile_cols - 1, 1),
            pltpu.roll(col_recv[step, 0], 1, 1),
        )

        own = lane % 2 == jnp.where(t == 0, 1, 0)
        if step < STEPS - 1:

            @pl.when(is_nest)
            def _():
                for p in range(2):
                    rim_copies(step, 0, p).wait_recv()
                outer[...] = rim_recv[step, 0] + rim_recv[step, 1]

                @pl.when(at_edge)
                def _():
                    for p in range(2):
                        side_copies(step, 0, p).wait_recv()
                    halo[...] = jnp.where(own, side_recv[step, 0] + side_recv[step, 1], halo[...])
        else:
            @pl.when(is_nest)
            def _():
                outer[...] = jnp.zeros_like(outer)

                @pl.when(at_edge)
                def _():
                    halo[...] = jnp.where(own, 0.0, halo[...])

        def update(v, u, sides):
            mate_row = row_recv[step, pl.ds(v, 1), :]
            outer_row = outer[pl.ds(v, 1), :]
            top = jnp.where(parity == 0, outer_row, mate_row)
            bottom = jnp.where(parity == 0, mate_row, outer_row)
            ghost = pltpu.roll(halo[...], tile_cols - 1 - 2 * v, 1)
            sides = sides + jnp.where((lane == 0) | (lane == tile_cols - 1), ghost, 0.0)
            above = jnp.where(row_id == 0, top, pltpu.roll(u, 1, 0))
            below = jnp.where(row_id == tile_rows - 1, bottom, pltpu.roll(u, tile_rows - 1, 0))
            laplace = above + below + sides - 4.0 * u
            new = u + diff_ref[...] * laplace
            target[v] = new
            if step + 1 < STEPS:
                take_edges(step + 1, v, new)

        def one(chunk, carry):
            cells = source[pl.ds(chunk * BATCH, BATCH)]
            sides = jnp.dot(
                split(cells.reshape(BATCH * tile_rows, tile_cols)), beside[...], preferred_element_type=jnp.float32
            )
            for j in range(BATCH):
                update(chunk * BATCH + j, cells[j], sides[j * tile_rows : (j + 1) * tile_rows])
            if step == STEPS - 1:

                @pl.when(is_parent)
                def _():
                    store(chunk).start()
            return carry

        lax.fori_loop(0, var_count // BATCH, one, 0)
        if step + 1 < STEPS:
            for copy in col_copies(step + 1):
                copy.start()

            @pl.when(is_parent)
            def _():
                interpolate(step + 1, target)

    @pl.when(is_nest)
    def _():
        last = STEPS - 1
        for p in range(2):
            rim_copies(last, 0, p).wait_recv()
        outer[...] = rim_recv[last, 0] + rim_recv[last, 1]

        def add_rims(chunk, row):
            for j in range(BATCH):
                v = chunk * BATCH + j
                u2[v, row : row + 1, :] = u2[v, row : row + 1, :] + diff_ref[row : row + 1] * outer[pl.ds(v, 1), :]

        def add_to_row(chunk):
            @pl.when(parity == 0)
            def _():
                add_rims(chunk, 0)

            @pl.when(parity == 1)
            def _():
                add_rims(chunk, tile_rows - 1)

        @pl.when(at_edge)
        def _():
            for p in range(2):
                side_copies(last, 0, p).wait_recv()
            own = lane % 2 == jnp.where(t == 0, 1, 0)
            halo[...] = jnp.where(own, side_recv[last, 0] + side_recv[last, 1], 0.0)

            def finish(chunk, carry):
                add_to_row(chunk)
                for j in range(BATCH):
                    v = chunk * BATCH + j
                    ghost = pltpu.roll(halo[...], tile_cols - 1 - 2 * v, 1)
                    ghost = jnp.where((lane == 0) | (lane == tile_cols - 1), ghost, 0.0)
                    u2[v] = u2[v] + diff_ref[...] * ghost
                store(chunk).start()
                return carry

            lax.fori_loop(0, var_count // BATCH, finish, 0)

        @pl.when(jnp.logical_not(at_edge))
        def _():
            def finish(chunk, carry):
                add_to_row(chunk)
                store(chunk).start()
                return carry

            lax.fori_loop(0, var_count // BATCH, finish, 0)

    for step in range(STEPS):
        for copy in col_copies(step):
            copy.wait_send()

    @pl.when(is_nest)
    def _():
        for p in range(2):
            for copy in param_copies(p, 0):
                copy.wait_send()

    @pl.when(is_parent)
    def _():
        for step in range(STEPS):
            for slot in range(nests):
                rim_copies(step, slot, 0).wait_send()

                @pl.when(at_edge)
                def _():
                    side_copies(step, slot, 0).wait_send()

    for chunk in range(var_count // BATCH):
        store(chunk).wait()


def per_device(mesh_shape, *arrays):
    model_state = arrays[0]
    var_count, tile_rows, tile_cols = model_state.shape
    blocks, columns = mesh_shape["nest"], mesh_shape["tx"]
    nests = blocks - 2
    f32 = jnp.float32
    tile = (tile_rows, tile_cols)
    rows = (var_count, tile_cols)
    smem = pl.BlockSpec(memory_space=pltpu.SMEM)
    hbm = pl.BlockSpec(memory_space=pltpu.HBM)
    dma = pltpu.SemaphoreType.DMA
    return pl.pallas_call(
        functools.partial(kernel, blocks, columns),
        out_shape=jax.ShapeDtypeStruct(model_state.shape, f32),
        in_specs=[hbm] * 6 + [smem] * 2,
        out_specs=hbm,
        scratch_shapes=[
            pltpu.VMEM(model_state.shape, f32),
            pltpu.VMEM(model_state.shape, f32),
            pltpu.VMEM(model_state.shape, f32),
            pltpu.VMEM(tile, f32),
            pltpu.VMEM((4, tile_cols), jnp.int32),
            pltpu.VMEM((4, tile_cols), f32),
            pltpu.VMEM((4, tile_cols), jnp.int32),
            pltpu.VMEM((4, tile_cols), f32),
            pltpu.VMEM((8, tile_cols), jnp.int32),
            pltpu.VMEM((2, 8, tile_cols), f32),
            pltpu.VMEM((nests, 8, tile_cols), jnp.int32),
            pltpu.VMEM((nests, 8, tile_cols), f32),
            pltpu.VMEM((nests // 2, 3, 4) + tile, f32),
            pltpu.VMEM((nests // 2, 3, 2 * tile_cols, 4 * tile_cols), jnp.bfloat16),
            pltpu.VMEM((2 * tile_cols, tile_cols), jnp.bfloat16),
            pltpu.VMEM((STEPS,) + tile, f32),
            pltpu.VMEM((STEPS, 2) + tile, f32),
            pltpu.VMEM(tile, f32),
            pltpu.VMEM((STEPS,) + rows, f32),
            pltpu.VMEM((STEPS,) + rows, f32),
            pltpu.VMEM(rows, f32),
            pltpu.VMEM((STEPS, nests) + rows, f32),
            pltpu.VMEM((STEPS, 2) + rows, f32),
            pltpu.VMEM((tile_cols, tile_cols), f32),
            pltpu.VMEM((STEPS, nests) + tile, f32),
            pltpu.VMEM((STEPS, 2) + tile, f32),
            dma((var_count // CHUNK,)),
            dma((5,)),
            dma((var_count // BATCH,)),
            dma((2, 2)),
            dma((2, nests)),
            dma((STEPS, 2)),
            dma((STEPS, 2)),
            dma((STEPS,)),
            dma((STEPS,)),
            dma((STEPS, nests)),
            dma((STEPS, 2)),
            dma((STEPS, nests)),
            dma((STEPS, 2)),
        ],
        compiler_params=pltpu.CompilerParams(
            collective_id=0, has_side_effects=True, vmem_limit_bytes=64 * 2**20
        ),
        cost_estimate=pl.CostEstimate(
            flops=20 * model_state.size, bytes_accessed=8 * model_state.size, transcendentals=0
        ),
    )(*arrays)


def solution(mesh):
    placed = (
        P("parts", "nest", "tx"),
        P(("parts", "nest"), "tx"),
        P("nest", "tx"),
        P("nest", "tx"),
        P("nest", None),
        P("nest", None),
        P("nest", "tx"),
        P(),
    )
    return jax.shard_map(
        functools.partial(per_device, dict(mesh.shape)),
        mesh=mesh,
        in_specs=placed,
        out_specs=P("parts", "nest", "tx"),
        check_vma=False,
    )
```

```python
import functools

import jax
import jax.numpy as jnp
from jax import lax
from jax.experimental import pallas as pl
from jax.experimental.pallas import tpu as pltpu
from jax.sharding import PartitionSpec as P

STEPS = 2
CHUNK = 8
BATCH = 8
PICK = 24
MESH = pl.DeviceIdType.MESH


def kernel(
    blocks,
    columns,
    state_hbm,
    diff_hbm,
    rim_index_hbm,
    rim_weight_hbm,
    side_index_hbm,
    side_weight_hbm,
    tile_ref,
    offset_ref,
    out_hbm,
    u0,
    u1,
    u2,
    diff_ref,
    rim_index_ref,
    rim_weight_ref,
    side_index_ref,
    side_weight_ref,
    idx_send,
    w_send,
    idx_recv,
    w_recv,
    row_weights,
    column_picks,
    beside,
    col_send,
    col_recv,
    halo,
    row_send,
    row_recv,
    outer,
    rim_out,
    rim_recv,
    side_rows,
    side_out,
    side_recv,
    load_sem,
    small_sem,
    store_sem,
    param_send_sem,
    param_recv_sem,
    col_send_sem,
    col_recv_sem,
    row_send_sem,
    row_recv_sem,
    rim_send_sem,
    rim_recv_sem,
    side_send_sem,
    side_recv_sem,
):
    var_count, tile_rows, tile_cols = u0.shape
    groups = tile_rows // 8
    nests = blocks - 2
    me = lax.axis_index("nest")
    t = lax.axis_index("tx")
    right, left = lax.rem(t + 1, columns), lax.rem(t + columns - 1, columns)
    parity = lax.rem(me, 2)
    mate = me + 1 - 2 * parity
    is_parent = me < 2
    is_nest = me >= 2
    at_edge = jnp.logical_or(t == 0, t == columns - 1)

    smalls = [
        pltpu.make_async_copy(source, target, small_sem.at[i])
        for i, (source, target) in enumerate(
            (
                (rim_index_hbm, rim_index_ref),
                (rim_weight_hbm, rim_weight_ref),
                (side_index_hbm, side_index_ref),
                (side_weight_hbm, side_weight_ref),
                (diff_hbm, diff_ref),
            )
        )
    ]
    for copy in smalls:
        copy.start()
    loads = [
        pltpu.make_async_copy(
            state_hbm.at[pl.ds(i * CHUNK, CHUNK)], u0.at[pl.ds(i * CHUNK, CHUNK)], load_sem.at[i]
        )
        for i in range(var_count // CHUNK)
    ]
    for copy in loads:
        copy.start()

    barrier = pltpu.get_barrier_semaphore()
    pl.semaphore_signal(barrier, inc=1, device_id={"tx": left}, device_id_type=MESH)
    pl.semaphore_signal(barrier, inc=1, device_id={"tx": right}, device_id_type=MESH)
    pl.semaphore_signal(barrier, inc=1, device_id={"nest": mate}, device_id_type=MESH)

    @pl.when(is_nest)
    def _():
        for p in range(2):
            pl.semaphore_signal(barrier, inc=1, device_id={"nest": p}, device_id_type=MESH)
        pl.semaphore_wait(barrier, 5)

    @pl.when(is_parent)
    def _():
        for b in range(nests):
            pl.semaphore_signal(barrier, inc=1, device_id={"nest": 2 + b}, device_id_type=MESH)
        pl.semaphore_wait(barrier, 3 + nests)

    row_id = lax.broadcasted_iota(jnp.int32, (tile_rows, tile_cols), 0)
    lane = lax.broadcasted_iota(jnp.int32, (tile_rows, tile_cols), 1)
    lane8 = lax.broadcasted_iota(jnp.int32, (8, tile_cols), 1)
    half = tile_rows

    def param_copies(p, slot):
        return (
            pltpu.make_async_remote_copy(
                src_ref=idx_send,
                dst_ref=idx_recv.at[slot],
                send_sem=param_send_sem.at[0, p],
                recv_sem=param_recv_sem.at[0, slot],
                device_id={"nest": p},
                device_id_type=MESH,
            ),
            pltpu.make_async_remote_copy(
                src_ref=w_send.at[p],
                dst_ref=w_recv.at[slot],
                send_sem=param_send_sem.at[1, p],
                recv_sem=param_recv_sem.at[1, slot],
                device_id={"nest": p},
                device_id_type=MESH,
            ),
        )

    for copy in smalls:
        copy.wait()

    @pl.when(is_nest)
    def _():
        offset = offset_ref[me // 2]
        tile = tile_ref[0, 0]
        stay = (t == 0) == (parity == 0)
        index = side_index_ref[...]
        weight = side_weight_ref[...]
        turned_index = jnp.concatenate([index[:, half:], index[:, :half]], axis=1)
        turned_weight = jnp.concatenate([weight[:, half:], weight[:, :half]], axis=1)
        idx_send[0:4] = rim_index_ref[...] + offset
        idx_send[4:8] = jnp.where(stay, index, turned_index) + offset
        for p in range(2):
            keep = jnp.where(tile == p, 1.0, 0.0)
            w_send[p, 0:4] = rim_weight_ref[...] * keep
            w_send[p, 4:8] = jnp.where(stay, weight, turned_weight) * keep
        for p in range(2):
            for copy in param_copies(p, me - 2):
                copy.start()

    def col_copies(step):
        return (
            pltpu.make_async_remote_copy(
                src_ref=col_send.at[step],
                dst_ref=col_recv.at[step, 0],
                send_sem=col_send_sem.at[step, 0],
                recv_sem=col_recv_sem.at[step, 0],
                device_id={"tx": right},
                device_id_type=MESH,
            ),
            pltpu.make_async_remote_copy(
                src_ref=col_send.at[step],
                dst_ref=col_recv.at[step, 1],
                send_sem=col_send_sem.at[step, 1],
                recv_sem=col_recv_sem.at[step, 1],
                device_id={"tx": left},
                device_id_type=MESH,
            ),
            pltpu.make_async_remote_copy(
                src_ref=row_send.at[step],
                dst_ref=row_recv.at[step],
                send_sem=row_send_sem.at[step],
                recv_sem=row_recv_sem.at[step],
                device_id={"nest": mate},
                device_id_type=MESH,
            ),
        )

    def take_edges(step, v, tile):
        last, first = tile[tile_rows - 1 :], tile[:1]
        row_send[step, pl.ds(v, 1), :] = jnp.where(parity == 0, last, first)
        outer[pl.ds(v, 1), :] = jnp.where(parity == 0, first, last)
        col_send[step] = jnp.where(lane // 2 == v, pltpu.roll(tile, 2 * v + 1, 1), col_send[step])

    col_send[...] = jnp.zeros_like(col_send)
    for i, copy in enumerate(loads):
        copy.wait()

        def first_edges(trip, carry):
            for j in range(BATCH):
                v = i * CHUNK + trip * BATCH + j
                take_edges(0, v, u0[v])
            return carry

        lax.fori_loop(0, CHUNK // BATCH, first_edges, 0)
    for copy in col_copies(0):
        copy.start()

    def rim_copies(step, slot, p):
        return pltpu.make_async_remote_copy(
            src_ref=rim_out.at[step, slot],
            dst_ref=rim_recv.at[step, p],
            send_sem=rim_send_sem.at[step, slot],
            recv_sem=rim_recv_sem.at[step, p],
            device_id={"nest": 2 + slot},
            device_id_type=MESH,
        )

    def side_copies(step, slot, p):
        return pltpu.make_async_remote_copy(
            src_ref=side_out.at[step, slot],
            dst_ref=side_recv.at[step, p],
            send_sem=side_send_sem.at[step, slot],
            recv_sem=side_recv_sem.at[step, p],
            device_id={"nest": 2 + slot},
            device_id_type=MESH,
        )

    def split(cells):
        high = cells.astype(jnp.bfloat16)
        low = (cells - high.astype(jnp.float32)).astype(jnp.bfloat16)
        return jnp.concatenate([high, low], axis=1)

    square = lax.broadcasted_iota(jnp.int32, (tile_cols, tile_cols), 0)

    def weights_of(index, weight):
        return jnp.where(row_id == index // tile_cols, weight, 0.0)

    def side_rows_of(pair):
        low = lane8[:4] < half
        index = jnp.where(low, idx_recv[2 * pair, 4:8], idx_recv[2 * pair + 1, 4:8])
        weight = jnp.where(low, w_recv[2 * pair, 4:8], w_recv[2 * pair + 1, 4:8])
        return index, weight

    def sets_of(pair, what):
        if what == 2:
            return side_rows_of(pair)
        return idx_recv[2 * pair + what, 0:4], w_recv[2 * pair + what, 0:4]

    def prepare():
        for slot in range(nests):
            for p in range(2):
                @pl.when(me == p)
                def _():
                    for copy in param_copies(p, slot):
                        copy.wait_recv()
        for pair in range(nests // 2):
            for what in range(3):
                index, weight = sets_of(pair, what)
                for k in range(4):
                    row_weights[pair, what, k] = weights_of(index[k : k + 1], weight[k : k + 1])
                    pick = jnp.where(square == lax.rem(index[k : k + 1], tile_cols), 1.0, 0.0).astype(jnp.bfloat16)
                    for part in range(2):
                        column_picks[
                            pair, what, part * tile_cols : (part + 1) * tile_cols, k * tile_cols : (k + 1) * tile_cols
                        ] = pick

    def interpolate(step, source):
        for pair in range(nests // 2):

            def run(whats):
                def one(trip, carry):
                    these = pl.ds(trip * PICK, PICK)
                    parts = split(source[these].reshape(PICK * tile_rows, tile_cols))
                    for what in whats:
                        total = jnp.zeros((PICK, 8, tile_cols), jnp.float32)
                        for two in range(2):
                            span = slice(2 * two * tile_cols, 2 * (two + 1) * tile_cols)
                            picked = jnp.dot(
                                parts, column_picks[pair, what, :, span], preferred_element_type=jnp.float32
                            )
                            for k in range(2):
                                one_k = picked[:, k * tile_cols : (k + 1) * tile_cols]
                                weighted = one_k.reshape(PICK, groups, 8, tile_cols) * row_weights[
                                    pair, what, 2 * two + k
                                ].reshape(1, groups, 8, tile_cols)
                                total = total + jnp.sum(weighted, axis=1)
                        value = jnp.sum(total, axis=1)
                        if what == 2:
                            side_rows[these, :] = value
                        else:
                            rim_out[step, 2 * pair + what, these, :] = value
                    return carry

                lax.fori_loop(0, var_count // PICK, one, 0)

            @pl.when(at_edge)
            def _():
                run((0, 1, 2))
                turned = side_rows[...].T
                for what in range(2):
                    side_out[step, 2 * pair + what] = jnp.take_along_axis(
                        turned[what * half : (what + 1) * half], lane // 2, axis=1, mode="promise_in_bounds"
                    )
                for what in range(2):
                    for p in range(2):
                        @pl.when(me == p)
                        def _():
                            side_copies(step, 2 * pair + what, p).start()

            @pl.when(jnp.logical_not(at_edge))
            def _():
                run((0, 1))

            for what in range(2):
                for p in range(2):
                    @pl.when(me == p)
                    def _():
                        rim_copies(step, 2 * pair + what, p).start()

    distance = square - lax.broadcasted_iota(jnp.int32, (tile_cols, tile_cols), 1)
    neighbours = jnp.where((distance == 1) | (distance == -1), 1.0, 0.0).astype(jnp.bfloat16)
    for part in range(2):
        beside[part * tile_cols : (part + 1) * tile_cols] = neighbours

    @pl.when(is_parent)
    def _():
        side_rows[...] = jnp.zeros_like(side_rows)
        prepare()
        interpolate(0, u0)

    def store(chunk):
        these = pl.ds(chunk * BATCH, BATCH)
        return pltpu.make_async_copy(u2.at[these], out_hbm.at[these], store_sem.at[chunk])

    for step in range(STEPS):
        source, target = ((u0, u1), (u1, u2))[step]
        to_right, to_left, to_mate = col_copies(step)
        to_right.wait_recv()
        to_left.wait_recv()
        to_mate.wait_recv()
        halo[...] = jnp.where(
            lane % 2 == 0,
            pltpu.roll(col_recv[step, 1], tile_cols - 1, 1),
            pltpu.roll(col_recv[step, 0], 1, 1),
        )

        @pl.when(is_nest)
        def _():
            for p in range(2):
                rim_copies(step, 0, p).wait_recv()
            outer[...] = rim_recv[step, 0] + rim_recv[step, 1]

            @pl.when(at_edge)
            def _():
                for p in range(2):
                    side_copies(step, 0, p).wait_recv()
                own = lane % 2 == jnp.where(t == 0, 1, 0)
                halo[...] = jnp.where(own, side_recv[step, 0] + side_recv[step, 1], halo[...])

        def update(v, u, sides):
            mate_row = row_recv[step, pl.ds(v, 1), :]
            outer_row = outer[pl.ds(v, 1), :]
            top = jnp.where(parity == 0, outer_row, mate_row)
            bottom = jnp.where(parity == 0, mate_row, outer_row)
            ghost = pltpu.roll(halo[...], tile_cols - 1 - 2 * v, 1)
            sides = sides + jnp.where((lane == 0) | (lane == tile_cols - 1), ghost, 0.0)
            above = jnp.where(row_id == 0, top, pltpu.roll(u, 1, 0))
            below = jnp.where(row_id == tile_rows - 1, bottom, pltpu.roll(u, tile_rows - 1, 0))
            laplace = above + below + sides - 4.0 * u
            new = u + diff_ref[...] * laplace
            target[v] = new
            if step + 1 < STEPS:
                take_edges(step + 1, v, new)

        def one(chunk, carry):
            cells = source[pl.ds(chunk * BATCH, BATCH)]
            sides = jnp.dot(
                split(cells.reshape(BATCH * tile_rows, tile_cols)), beside[...], preferred_element_type=jnp.float32
            )
            for j in range(BATCH):
                update(chunk * BATCH + j, cells[j], sides[j * tile_rows : (j + 1) * tile_rows])
            if step == STEPS - 1:
                store(chunk).start()
            return carry

        lax.fori_loop(0, var_count // BATCH, one, 0)
        if step + 1 < STEPS:
            for copy in col_copies(step + 1):
                copy.start()

            @pl.when(is_parent)
            def _():
                interpolate(step + 1, target)

    for step in range(STEPS):
        for copy in col_copies(step):
            copy.wait_send()

    @pl.when(is_nest)
    def _():
        for p in range(2):
            for copy in param_copies(p, 0):
                copy.wait_send()

    @pl.when(is_parent)
    def _():
        for step in range(STEPS):
            for slot in range(nests):
                rim_copies(step, slot, 0).wait_send()

                @pl.when(at_edge)
                def _():
                    side_copies(step, slot, 0).wait_send()

    for chunk in range(var_count // BATCH):
        store(chunk).wait()


def per_device(mesh_shape, *arrays):
    model_state = arrays[0]
    var_count, tile_rows, tile_cols = model_state.shape
    blocks, columns = mesh_shape["nest"], mesh_shape["tx"]
    nests = blocks - 2
    f32 = jnp.float32
    tile = (tile_rows, tile_cols)
    rows = (var_count, tile_cols)
    smem = pl.BlockSpec(memory_space=pltpu.SMEM)
    hbm = pl.BlockSpec(memory_space=pltpu.HBM)
    dma = pltpu.SemaphoreType.DMA
    return pl.pallas_call(
        functools.partial(kernel, blocks, columns),
        out_shape=jax.ShapeDtypeStruct(model_state.shape, f32),
        in_specs=[hbm] * 6 + [smem] * 2,
        out_specs=hbm,
        scratch_shapes=[
            pltpu.VMEM(model_state.shape, f32),
            pltpu.VMEM(model_state.shape, f32),
            pltpu.VMEM(model_state.shape, f32),
            pltpu.VMEM(tile, f32),
            pltpu.VMEM((4, tile_cols), jnp.int32),
            pltpu.VMEM((4, tile_cols), f32),
            pltpu.VMEM((4, tile_cols), jnp.int32),
            pltpu.VMEM((4, tile_cols), f32),
            pltpu.VMEM((8, tile_cols), jnp.int32),
            pltpu.VMEM((2, 8, tile_cols), f32),
            pltpu.VMEM((nests, 8, tile_cols), jnp.int32),
            pltpu.VMEM((nests, 8, tile_cols), f32),
            pltpu.VMEM((nests // 2, 3, 4) + tile, f32),
            pltpu.VMEM((nests // 2, 3, 2 * tile_cols, 4 * tile_cols), jnp.bfloat16),
            pltpu.VMEM((2 * tile_cols, tile_cols), jnp.bfloat16),
            pltpu.VMEM((STEPS,) + tile, f32),
            pltpu.VMEM((STEPS, 2) + tile, f32),
            pltpu.VMEM(tile, f32),
            pltpu.VMEM((STEPS,) + rows, f32),
            pltpu.VMEM((STEPS,) + rows, f32),
            pltpu.VMEM(rows, f32),
            pltpu.VMEM((STEPS, nests) + rows, f32),
            pltpu.VMEM((STEPS, 2) + rows, f32),
            pltpu.VMEM((tile_cols, tile_cols), f32),
            pltpu.VMEM((STEPS, nests) + tile, f32),
            pltpu.VMEM((STEPS, 2) + tile, f32),
            dma((var_count // CHUNK,)),
            dma((5,)),
            dma((var_count // BATCH,)),
            dma((2, 2)),
            dma((2, nests)),
            dma((STEPS, 2)),
            dma((STEPS, 2)),
            dma((STEPS,)),
            dma((STEPS,)),
            dma((STEPS, nests)),
            dma((STEPS, 2)),
            dma((STEPS, nests)),
            dma((STEPS, 2)),
        ],
        compiler_params=pltpu.CompilerParams(
            collective_id=0, has_side_effects=True, vmem_limit_bytes=64 * 2**20
        ),
        cost_estimate=pl.CostEstimate(
            flops=20 * model_state.size, bytes_accessed=8 * model_state.size, transcendentals=0
        ),
    )(*arrays)


def solution(mesh):
    placed = (
        P("parts", "nest", "tx"),
        P(("parts", "nest"), "tx"),
        P("nest", "tx"),
        P("nest", "tx"),
        P("nest", None),
        P("nest", None),
        P("nest", "tx"),
        P(),
    )
    return jax.shard_map(
        functools.partial(per_device, dict(mesh.shape)),
        mesh=mesh,
        in_specs=placed,
        out_specs=P("parts", "nest", "tx"),
        check_vma=False,
    )
```
